256 devices in a mesh: tm: 16 (over z, core), space: 16 (over x, y).
Axes of the slice: x: 4, y: 4, z: 8, core: 2. Of those that a mesh axis runs over, the one named last changes fastest.
Arguments:
- initial: float32 [96, 128, 128], P('space'), may hold values from -6 to 6
- guess: float32 [16, 96, 128, 128], P('tm', 'space'), may hold values from -6 to 6
- courant: float32 [3, 96, 128, 128], P(None, 'space'), may hold values from -0.08 to 0.08
- diffusion: float32 [96, 128, 128], P('space'), may hold values from 0.05 to 1
- inflow: float32 [96, 128, 128], P('space'), may hold values from -6 to 6
Outputs:
- corrected: float32 [16, 96, 128, 128], P('tm', 'space')
- residual: float32 [16, 96, 128, 128], P('tm', 'space')
The draws below stay inside these ranges and needn't reach their ends.
All inputs are finite; a program needn't handle non-finite values.
Results may differ from the reference program's by a relative error of at most 0.000033.
Values sent between devices are 32-bit elements; how exact they have to be, the bound alone decides.
No kernel may reach another device: no remote copies, remote signals or barrier semaphores. Data moves between devices by JAX's collectives and lax.ppermute only.
A program may use at most 64 MiB of HBM per device.

```python
import math
import jax
import jax.numpy as jnp

X = 128
Y = 128
STEPS_DEV = 4
SWEEPS = 4
NZ = 96
INTERVALS = 16


def clipped_normal(key, leading):
    full_shape = leading + (NZ, X, Y)
    return jnp.clip(jax.random.normal(key, full_shape, jnp.float32), -6.0, 6.0)


def draw_initial(key, part):
    key = jax.random.fold_in(key, 11)
    return clipped_normal(key, ())


def draw_guess(key, part):
    key = jax.random.fold_in(key, 23)
    return clipped_normal(key, (INTERVALS,))


def draw_inflow(key, part):
    key = jax.random.fold_in(key, 37)
    return clipped_normal(key, ())


def shard_levels(rng, extent, shards, least, largest):
    factor_of, own = 1.0, jax.random.fold_in(rng, 6)
    for axis_at, parts in shards:
        draws = jnp.exp(jax.random.uniform(jax.random.fold_in(own, axis_at), (parts,), jnp.float32, least / len(shards), largest / len(shards)))
        factor_of = factor_of * jnp.repeat(draws, extent[axis_at] // parts).reshape([-1 if axis == axis_at else 1 for axis in range(len(extent))])
    return factor_of


def setup_inputs(seed: int = 0) -> dict:
    key_list = jax.random.split(jax.random.key(seed), 6)
    initial = draw_initial(jax.random.fold_in(key_list[5], 71), 0)
    guess = draw_guess(jax.random.fold_in(key_list[5], 71), 0)
    courant = jnp.clip(jax.random.uniform(key_list[2], (3, NZ, X, Y), jnp.float32, -0.08, 0.08) * shard_levels(key_list[2], (3, NZ, X, Y), ((1, 16),), -0.4, 0.0), -0.08, 0.08)
    diffusion = jnp.clip(jnp.exp(math.log(1.0) - 2.9957323 * jax.random.uniform(key_list[3], (NZ, X, Y), jnp.float32) ** shard_levels(key_list[3], (NZ, X, Y), ((0, 16),), -0.2, 0.2)), 0.05, 1.0)
    inflow = draw_inflow(jax.random.fold_in(key_list[5], 71), 0)
    return {"initial": initial, "guess": guess, "courant": courant, "diffusion": diffusion, "inflow": inflow}


def upwind(speed, centre, below, above):
    return jnp.maximum(speed, 0.0) * (centre - below) + jnp.minimum(speed, 0.0) * (above - centre)


def neighbor_sum(field):
    padded = jnp.pad(field, [(0, 0)] * (field.ndim - 3) + [(1, 1)] * 3)
    summed = padded[..., 2:, 1:-1, 1:-1] + padded[..., :-2, 1:-1, 1:-1]
    summed = summed + padded[..., 1:-1, 2:, 1:-1] + padded[..., 1:-1, :-2, 1:-1]
    return summed + padded[..., 1:-1, 1:-1, 2:] + padded[..., 1:-1, 1:-1, :-2]


def advance(state, courant, diffusion, factor):
    padded = jnp.pad(state, [(0, 0)] * (state.ndim - 3) + [(1, 1)] * 3)
    transport = upwind(courant[0], state, padded[..., :-2, 1:-1, 1:-1], padded[..., 2:, 1:-1, 1:-1])
    transport = transport + upwind(courant[1], state, padded[..., 1:-1, :-2, 1:-1], padded[..., 1:-1, 2:, 1:-1])
    transport = transport + upwind(courant[2], state, padded[..., 1:-1, 1:-1, :-2], padded[..., 1:-1, 1:-1, 2:])
    source = state - factor * transport
    scaled = factor * diffusion
    diagonal = 1.0 + 6.0 * scaled
    iterate = source
    for sweep in range(SWEEPS):
        iterate = (source + scaled * neighbor_sum(iterate)) / diagonal
    return iterate


def reference(initial, guess, courant, diffusion, inflow):
    def previous(points):
        return jnp.concatenate([initial[None], points[:-1]], axis=0)

    def relax(points):
        state = previous(points)
        for step in range(STEPS_DEV - 1):
            state = advance(state, courant, diffusion, 1.0)
        return advance(state, courant, diffusion, 1.0)

    relaxed = relax(guess)
    residual = relax(relaxed) - relaxed
    error = inflow.astype(jnp.float32)
    errors = []
    for interval in range(INTERVALS):
        error = advance(error, courant, diffusion, float(STEPS_DEV)) + residual[interval]
        errors.append(error)
    corrected = relaxed + jnp.stack(errors, axis=0)
    return corrected, residual
```

```python
import functools

import jax
import jax.numpy as jnp
from jax import lax
from jax.experimental import pallas as pl
from jax.experimental.pallas import tpu as pltpu
from jax.sharding import PartitionSpec as P

STEPS_DEV = 4
SWEEPS = 4
SUB = 8
LANES = 128
VMEM_LIMIT = 24 * 2**20
F32 = jnp.float32


def split_rows(cells):
    rows = cells.shape[-2] // SUB
    shaped = cells.reshape(cells.shape[:-2] + (SUB, rows, LANES))
    return jnp.swapaxes(shaped, -3, -2)


def join_rows(cells):
    rows = cells.shape[-3]
    return jnp.swapaxes(cells, -3, -2).reshape(cells.shape[:-3] + (rows * SUB, LANES))


def shapes(planes, rows):
    return jax.ShapeDtypeStruct((planes, rows, SUB, LANES), F32)


VMEM = pl.BlockSpec(memory_space=pltpu.VMEM)
SMEM = pl.BlockSpec(memory_space=pltpu.SMEM)
PARAMS = pltpu.CompilerParams(vmem_limit_bytes=VMEM_LIMIT)


def prepare(info, stacked, mine, other):
    slab, rows = stacked.shape[1], stacked.shape[2]
    wide, narrow = slab + 8, slab + 6

    def kernel(info_ref, own_ref, mine_ref, other_ref, cou_ref, a1, i1, a4, i4, q_ref):
        core = info_ref[0]
        low = info_ref[1].astype(F32)
        high = info_ref[2].astype(F32)

        def place(field, refs, index):
            into = (lambda p, value: cou_ref.__setitem__((field, p), value)) if field < 3 else (
                lambda p, value: q_ref.__setitem__(p, value)
            )
            for p in range(4):
                into(p, refs[0, index, p] * low)
                into(slab + 4 + p, refs[1, index, p] * high)

        for p in range(slab):
            for field in range(3):
                cou_ref[field, p + 4] = own_ref[field, p]
            q_ref[p + 4] = own_ref[3, p]

        @pl.when(core == 0)
        def _():
            for field in range(4):
                place(field, mine_ref if field < 2 else other_ref, field % 2)

        @pl.when(core == 1)
        def _():
            for field in range(4):
                place(field, other_ref if field < 2 else mine_ref, field % 2)

        for p in range(narrow):
            scale = low if p < 3 else (high if p >= slab + 3 else 1.0)
            for factor, a_ref, i_ref in ((1.0, a1, i1), (float(STEPS_DEV), a4, i4)):
                q = factor * q_ref[p + 1]
                inverse = scale / (1.0 + 6.0 * q)
                i_ref[p] = inverse
                a_ref[p] = q * inverse

    return pl.pallas_call(
        kernel,
        out_shape=(jax.ShapeDtypeStruct((3, wide, rows, SUB, LANES), F32),) + (shapes(narrow, rows),) * 4,
        in_specs=[SMEM, VMEM, VMEM, VMEM],
        out_specs=(VMEM,) * 5,
        scratch_shapes=[pltpu.VMEM((wide, rows, SUB, LANES), F32)],
        compiler_params=PARAMS,
        name="prepare",
    )(info, stacked, mine, other)


@functools.partial(jax.jit, static_argnames=("factor", "kind"))
def step(info, own, lower, upper, courant, a, inverse, factor, extra=None, kind="plain"):
    slab, rows = own.shape[0], own.shape[1]
    edge = SWEEPS + 1
    total = slab + 2 * edge

    def kernel(info_ref, own_ref, lo_ref, hi_ref, cou, a_ref, inv_ref, *rest):
        if kind == "plain":
            out, head, tail, u, v, w, b = rest
        elif kind == "less":
            extra_ref, out, u, v, w, b = rest
        else:
            extra_ref, out, head, tail, slot, u, v, w, b = rest
        lane = lax.broadcasted_iota(jnp.int32, (SUB, LANES), 1)
        sub = lax.broadcasted_iota(jnp.int32, (SUB, LANES), 0)
        first_lane, last_lane = lane == 0, lane == LANES - 1
        first_sub, last_sub = sub == 0, sub == SUB - 1
        low = info_ref[1].astype(F32)
        high = info_ref[2].astype(F32)

        def sides(x):
            left = jnp.where(first_lane, 0.0, pltpu.roll(x, 1, 1))
            right = jnp.where(last_lane, 0.0, pltpu.roll(x, LANES - 1, 1))
            return left, right

        def column(ref, z):
            xs = [ref[z, r] for r in range(rows)]
            top = jnp.where(first_sub, 0.0, pltpu.roll(xs[-1], 1, 0))
            bottom = jnp.where(last_sub, 0.0, pltpu.roll(xs[0], SUB - 1, 0))
            return [top] + xs + [bottom]

        for p in range(edge):
            u[p] = lo_ref[p] * low
            u[edge + slab + p] = hi_ref[p] * high
        for p in range(slab):
            u[edge + p] = own_ref[p]

        for z in range(1, total - 1):
            xs = column(u, z)
            for r in range(rows):
                x = xs[r + 1]
                left, right = sides(x)
                c = cou[0, z - 1, r]
                t = c * jnp.where(c > 0.0, x - u[z - 1, r], u[z + 1, r] - x)
                c = cou[1, z - 1, r]
                t = t + c * jnp.where(c > 0.0, x - xs[r], xs[r + 2] - x)
                c = cou[2, z - 1, r]
                t = t + c * jnp.where(c > 0.0, x - left, right - x)
                v[z, r] = x - factor * t

        src, dst = v, w
        for k in range(SWEEPS):
            for z in range(2 + k, total - 2 - k):
                xs = column(src, z)
                for r in range(rows):
                    x = xs[r + 1]
                    left, right = sides(x)
                    around = (left + right) + (xs[r] + xs[r + 2]) + (src[z - 1, r] + src[z + 1, r])
                    if k == 0:
                        base = inv_ref[z - 2, r] * x
                        b[z - 2, r] = base
                    else:
                        base = b[z - 2, r]
                    value = base + a_ref[z - 2, r] * around
                    if k < SWEEPS - 1:
                        dst[z, r] = value
                        continue
                    p = z - edge
                    if kind == "less":
                        value = value - extra_ref[p, r]
                    elif kind == "ring":
                        value = value + extra_ref[p, r]
                    out[p, r] = value
                    if kind != "less":
                        if p < edge:
                            head[p, r] = value
                        if p >= slab - edge:
                            tail[p - (slab - edge), r] = value
            src, dst = dst, src

        if kind == "ring":
            at_start = info_ref[3] == 1

            @pl.when(at_start)
            def _():
                slot[...] = out[...]

            @pl.when(jnp.logical_not(at_start))
            def _():
                slot[...] = extra_ref[...]

    outs = [shapes(slab, rows)]
    if kind != "less":
        outs += [shapes(edge, rows)] * 2
    if kind == "ring":
        outs += [shapes(slab, rows)]
    operands = [info, own, lower, upper, courant, a, inverse] + ([] if extra is None else [extra])
    return pl.pallas_call(
        kernel,
        out_shape=tuple(outs),
        in_specs=[SMEM] + [VMEM] * (len(operands) - 1),
        out_specs=(VMEM,) * len(outs),
        scratch_shapes=[pltpu.VMEM((total, rows, SUB, LANES), F32)] * 3
        + [pltpu.VMEM((total - 4, rows, SUB, LANES), F32)],
        compiler_params=PARAMS,
        name="step_" + kind,
    )(*operands)


def per_device(initial, guess, courant, diffusion, inflow):
    slabs = lax.axis_size("space")
    points = lax.axis_size("tm")
    edge = SWEEPS + 1
    up = [(i, (i + 1) % slabs) for i in range(slabs)]
    down = [((i + 1) % slabs, i) for i in range(slabs)]
    later = [(i, (i + 1) % points) for i in range(points)]
    earlier = [((i + 1) % points, i) for i in range(points)]
    partner = [(i, i ^ 1) for i in range(points)]

    place = lax.axis_index("space")
    time_place = lax.axis_index("tm")
    core = time_place % 2
    at_start = time_place == 0
    info = jnp.stack([core, place > 0, place < slabs - 1, at_start]).astype(jnp.int32)

    def halos(head, tail):
        return lax.ppermute(tail, "space", up), lax.ppermute(head, "space", down)

    source = split_rows(jnp.where(time_place == points - 1, initial, guess[0]))
    state = lax.ppermute(source, "tm", later)

    stacked = split_rows(jnp.concatenate([courant, diffusion[None]], axis=0))
    half = lax.dynamic_slice_in_dim(stacked, 2 * core, 2, axis=0)
    lower, upper = halos(half[:, :4], half[:, half.shape[1] - 4 :])
    mine = jnp.stack([lower, upper])
    other = lax.ppermute(mine, "tm", partner)
    cou, a1, i1, a4, i4 = prepare(info, stacked, mine, other)

    slab = state.shape[0]
    lo, hi = halos(state[:edge], state[slab - edge :])
    for turn in range(STEPS_DEV):
        state, head, tail = step(info, state, lo, hi, cou, a1, i1, 1.0)
        lo, hi = halos(head, tail)
    relaxed = state
    relaxed_later = lax.ppermute(relaxed, "tm", earlier)
    for turn in range(STEPS_DEV - 1):
        state, head, tail = step(info, state, lo, hi, cou, a1, i1, 1.0)
        lo, hi = halos(head, tail)
    (slot,) = step(info, state, lo, hi, cou, a1, i1, 1.0, relaxed_later, "less")

    second_pass = relaxed
    first_residual = second_pass - relaxed
    residual = jnp.where(at_start, first_residual, lax.ppermute(slot, "tm", later))

    coarse = float(STEPS_DEV)
    inflow = split_rows(inflow)
    lo, hi = halos(inflow[:edge], inflow[slab - edge :])
    error, head, tail, _ = step(info, inflow, lo, hi, cou, a4, i4, coarse, first_residual, "ring")
    first_error = error
    for turn in range(1, points):
        lo, hi = halos(head, tail)
        error, head, tail, slot = step(info, error, lo, hi, cou, a4, i4, coarse, slot, "ring")
        slot = lax.ppermute(slot, "tm", earlier)
    corrected = relaxed + jnp.where(at_start, first_error, slot)
    return join_rows(corrected)[None], join_rows(residual)[None]


def solution(mesh):
    in_specs = (
        P("space", None, None),
        P("tm", "space", None, None),
        P(None, "space", None, None),
        P("space", None, None),
        P("space", None, None),
    )
    out_specs = (P("tm", "space", None, None), P("tm", "space", None, None))
    return jax.shard_map(
        per_device, mesh=mesh, in_specs=in_specs, out_specs=out_specs, check_vma=False
    )
```

```python
import functools

import jax
import jax.numpy as jnp
from jax import lax
from jax.experimental import pallas as pl
from jax.experimental.pallas import tpu as pltpu
from jax.sharding import PartitionSpec as P

STEPS_DEV = 4
SWEEPS = 4
SUB = 8
LANES = 128
VMEM_LIMIT = 24 * 2**20
F32 = jnp.float32


def split_rows(cells):
    rows = cells.shape[-2] // SUB
    shaped = cells.reshape(cells.shape[:-2] + (SUB, rows, LANES))
    return jnp.swapaxes(shaped, -3, -2)


def join_rows(cells):
    rows = cells.shape[-3]
    return jnp.swapaxes(cells, -3, -2).reshape(cells.shape[:-3] + (rows * SUB, LANES))


def shapes(planes, rows):
    return jax.ShapeDtypeStruct((planes, rows, SUB, LANES), F32)


VMEM = pl.BlockSpec(memory_space=pltpu.VMEM)
SMEM = pl.BlockSpec(memory_space=pltpu.SMEM)
PARAMS = pltpu.CompilerParams(vmem_limit_bytes=VMEM_LIMIT)


def prepare(info, stacked, mine, other):
    slab, rows = stacked.shape[1], stacked.shape[2]
    wide, narrow = slab + 8, slab + 6

    def kernel(info_ref, own_ref, mine_ref, other_ref, cou_ref, a1, i1, a4, i4, q_ref):
        core = info_ref[0]
        low = info_ref[1].astype(F32)
        high = info_ref[2].astype(F32)

        def place(field, refs, index):
            into = (lambda p, value: cou_ref.__setitem__((field, p), value)) if field < 3 else (
                lambda p, value: q_ref.__setitem__(p, value)
            )
            for p in range(4):
                into(p, refs[0, index, p] * low)
                into(slab + 4 + p, refs[1, index, p] * high)

        for p in range(slab):
            for field in range(3):
                cou_ref[field, p + 4] = own_ref[field, p]
            q_ref[p + 4] = own_ref[3, p]

        @pl.when(core == 0)
        def _():
            for field in range(4):
                place(field, mine_ref if field < 2 else other_ref, field % 2)

        @pl.when(core == 1)
        def _():
            for field in range(4):
                place(field, other_ref if field < 2 else mine_ref, field % 2)

        for p in range(narrow):
            scale = low if p < 3 else (high if p >= slab + 3 else 1.0)
            for factor, a_ref, i_ref in ((1.0, a1, i1), (float(STEPS_DEV), a4, i4)):
                q = factor * q_ref[p + 1]
                inverse = scale / (1.0 + 6.0 * q)
                i_ref[p] = inverse
                a_ref[p] = q * inverse

    return pl.pallas_call(
        kernel,
        out_shape=(jax.ShapeDtypeStruct((3, wide, rows, SUB, LANES), F32),) + (shapes(narrow, rows),) * 4,
        in_specs=[SMEM, VMEM, VMEM, VMEM],
        out_specs=(VMEM,) * 5,
        scratch_shapes=[pltpu.VMEM((wide, rows, SUB, LANES), F32)],
        compiler_params=PARAMS,
        name="prepare",
    )(info, stacked, mine, other)


@functools.partial(jax.jit, static_argnames=("factor", "kind"))
def step(info, own, lower, upper, courant, a, inverse, factor, extra=None, kind="plain"):
    slab, rows = own.shape[0], own.shape[1]
    edge = SWEEPS + 1
    total = slab + 2 * edge

    def kernel(info_ref, own_ref, lo_ref, hi_ref, cou, a_ref, inv_ref, *rest):
        if kind == "plain":
            out, head, tail, u, v, w, b = rest
        elif kind == "less":
            extra_ref, out, u, v, w, b = rest
        else:
            extra_ref, out, head, tail, slot, u, v, w, b = rest
        lane = lax.broadcasted_iota(jnp.int32, (SUB, LANES), 1)
        sub = lax.broadcasted_iota(jnp.int32, (SUB, LANES), 0)
        first_lane, last_lane = lane == 0, lane == LANES - 1
        first_sub, last_sub = sub == 0, sub == SUB - 1
        low = info_ref[1].astype(F32)
        high = info_ref[2].astype(F32)

        def sides(x):
            left = jnp.where(first_lane, 0.0, pltpu.roll(x, 1, 1))
            right = jnp.where(last_lane, 0.0, pltpu.roll(x, LANES - 1, 1))
            return left, right

        def column(ref, z):
            xs = [ref[z, r] for r in range(rows)]
            top = jnp.where(first_sub, 0.0, pltpu.roll(xs[-1], 1, 0))
            bottom = jnp.where(last_sub, 0.0, pltpu.roll(xs[0], SUB - 1, 0))
            return [top] + xs + [bottom]

        for p in range(edge):
            u[p] = lo_ref[p] * low
            u[edge + slab + p] = hi_ref[p] * high
        for p in range(slab):
            u[edge + p] = own_ref[p]

        for z in range(1, total - 1):
            xs = column(u, z)
            for r in range(rows):
                x = xs[r + 1]
                left, right = sides(x)
                c = cou[0, z - 1, r]
                t = c * jnp.where(c > 0.0, x - u[z - 1, r], u[z + 1, r] - x)
                c = cou[1, z - 1, r]
                t = t + c * jnp.where(c > 0.0, x - xs[r], xs[r + 2] - x)
                c = cou[2, z - 1, r]
                t = t + c * jnp.where(c > 0.0, x - left, right - x)
                v[z, r] = x - factor * t

        src, dst = v, w
        for k in range(SWEEPS):
            for z in range(2 + k, total - 2 - k):
                xs = column(src, z)
                for r in range(rows):
                    x = xs[r + 1]
                    left, right = sides(x)
                    around = (left + right) + (xs[r] + xs[r + 2]) + (src[z - 1, r] + src[z + 1, r])
                    if k == 0:
                        base = inv_ref[z - 2, r] * x
                        b[z - 2, r] = base
                    else:
                        base = b[z - 2, r]
                    value = base + a_ref[z - 2, r] * around
                    if k < SWEEPS - 1:
                        dst[z, r] = value
                        continue
                    p = z - edge
                    if kind == "less":
                        value = value - extra_ref[p, r]
                    elif kind == "ring":
                        value = value + extra_ref[p, r]
                    out[p, r] = value
                    if kind != "less":
                        if p < edge:
                            head[p, r] = value
                        if p >= slab - edge:
                            tail[p - (slab - edge), r] = value
            src, dst = dst, src

        if kind == "ring":
            at_start = info_ref[3] == 1

            @pl.when(at_start)
            def _():
                slot[...] = out[...]

            @pl.when(jnp.logical_not(at_start))
            def _():
                slot[...] = extra_ref[...]

    outs = [shapes(slab, rows)]
    if kind != "less":
        outs += [shapes(edge, rows)] * 2
    if kind == "ring":
        outs += [shapes(slab, rows)]
    operands = [info, own, lower, upper, courant, a, inverse] + ([] if extra is None else [extra])
    return pl.pallas_call(
        kernel,
        out_shape=tuple(outs),
        in_specs=[SMEM] + [VMEM] * (len(operands) - 1),
        out_specs=(VMEM,) * len(outs),
        scratch_shapes=[pltpu.VMEM((total, rows, SUB, LANES), F32)] * 3
        + [pltpu.VMEM((total - 4, rows, SUB, LANES), F32)],
        compiler_params=PARAMS,
        cost_estimate=pl.CostEstimate(flops=16 * 2**20, bytes_accessed=6 * 2**20, transcendentals=0),
        name="step_" + kind,
    )(*operands)


def routes(points, slabs):
    def route(move):
        pairs = []
        for t in range(points):
            for s in range(slabs):
                to_t, to_s = move(t, s)
                pairs.append((t * slabs + s, (to_t % points) * slabs + to_s % slabs))
        return pairs

    def halo_of_start(shift, cycle):
        def move(t, s):
            if t == 0:
                return 0, s + shift
            return cycle.get(t, t ^ 1), s

        return route(move)

    ahead = {1: 2, 2: 3, 3: 1}
    behind = {1: points - 2, points - 2: points - 1, points - 1: 1}
    return {
        "later": route(lambda t, s: (t + 1, s)),
        "later_up": route(lambda t, s: (t + 1, s + 1)),
        "later_down": route(lambda t, s: (t + 1, s - 1)),
        "start_up": halo_of_start(1, ahead),
        "start_down": halo_of_start(-1, behind),
    }


def per_device(initial, guess, courant, diffusion, inflow):
    slabs = lax.axis_size("space")
    points = lax.axis_size("tm")
    edge = SWEEPS + 1
    both = ("tm", "space")
    route = routes(points, slabs)
    up = [(i, (i + 1) % slabs) for i in range(slabs)]
    down = [((i + 1) % slabs, i) for i in range(slabs)]
    earlier = [((i + 1) % points, i) for i in range(points)]
    partner = [(i, i ^ 1) for i in range(points)]
    ring = [(i, (i - 2 if i % 2 == 0 else i + 2) % points) for i in range(points)]
    leave = [(i, (i - 1 if i % 2 == 0 else i + 1) % points) for i in range(points)]

    place = lax.axis_index("space")
    time_place = lax.axis_index("tm")
    core = time_place % 2
    at_start = time_place == 0
    info = jnp.stack([core, place > 0, place < slabs - 1, at_start]).astype(jnp.int32)

    def halos(head, tail):
        return lax.ppermute(tail, "space", up), lax.ppermute(head, "space", down)

    def start_halos(head, tail):
        return (
            lax.ppermute(tail, both, route["start_up"]),
            lax.ppermute(head, both, route["start_down"]),
        )

    source = split_rows(jnp.where(time_place == points - 1, initial, guess[0]))
    slab = source.shape[0]

    stacked = split_rows(jnp.concatenate([courant, diffusion[None]], axis=0))
    half = lax.dynamic_slice_in_dim(stacked, 2 * core, 2, axis=0)
    half, source = lax.optimization_barrier((half, source))
    state = lax.ppermute(source, both, route["later"])
    lo = lax.ppermute(source[slab - edge :], both, route["later_up"])
    hi = lax.ppermute(source[:edge], both, route["later_down"])
    mine = jnp.stack(halos(half[:, :4], half[:, slab - 4 :]))
    other = lax.ppermute(mine, "tm", partner)
    cou, a1, i1, a4, i4 = prepare(info, stacked, mine, other)

    inflow = split_rows(inflow)
    error_lo, error_hi = start_halos(inflow[:edge], inflow[slab - edge :])

    for turn in range(STEPS_DEV):
        state, head, tail = step(info, state, lo, hi, cou, a1, i1, 1.0)
        lo, hi = halos(head, tail)
        if turn == 0:
            lo, hi, error_lo, error_hi = lax.optimization_barrier((lo, hi, error_lo, error_hi))
    relaxed = state
    relaxed_later = lax.ppermute(relaxed, "tm", earlier)

    second_pass = relaxed
    first_residual = second_pass - relaxed
    coarse = float(STEPS_DEV)
    error, head, tail, _ = step(
        info, inflow, error_lo, error_hi, cou, a4, i4, coarse, first_residual, "ring"
    )
    first_error = error
    error_lo, error_hi = start_halos(head, tail)

    for turn in range(STEPS_DEV - 1):
        state, head, tail = step(info, state, lo, hi, cou, a1, i1, 1.0)
        lo, hi = halos(head, tail)
    lo, hi, error_lo, error_hi = lax.optimization_barrier((lo, hi, error_lo, error_hi))
    (odd,) = step(info, state, lo, hi, cou, a1, i1, 1.0, relaxed_later, "less")
    even = lax.ppermute(odd, "tm", earlier)
    residual = lax.ppermute(odd, both, route["later"])

    for turn in range(1, points):
        slot = odd if turn % 2 else even
        error, head, tail, slot = step(
            info, error, error_lo, error_hi, cou, a4, i4, coarse, slot, "ring"
        )
        if turn < points - 1:
            error_lo, error_hi = start_halos(head, tail)
            if turn == 3:
                residual, slot, error_lo, error_hi = lax.optimization_barrier(
                    (residual, slot, error_lo, error_hi)
                )
            else:
                slot, error_lo, error_hi = lax.optimization_barrier((slot, error_lo, error_hi))
            slot = lax.ppermute(slot, "tm", ring)
        else:
            slot = lax.ppermute(slot, "tm", leave)
        if turn % 2:
            odd = slot
        else:
            even = slot
    residual = jnp.where(at_start, first_residual, residual)
    error = jnp.where(at_start, first_error, jnp.where(core == 1, odd, even))
    return join_rows(relaxed + error)[None], join_rows(residual)[None]


def solution(mesh):
    in_specs = (
        P("space", None, None),
        P("tm", "space", None, None),
        P(None, "space", None, None),
        P("space", None, None),
        P("space", None, None),
    )
    out_specs = (P("tm", "space", None, None), P("tm", "space", None, None))
    return jax.shard_map(
        per_device, mesh=mesh, in_specs=in_specs, out_specs=out_specs, check_vma=False
    )
```

```python
import functools

import jax
import jax.numpy as jnp
from jax import lax
from jax.experimental import pallas as pl
from jax.experimental.pallas import tpu as pltpu
from jax.sharding import PartitionSpec as P

STEPS_DEV = 4
SWEEPS = 4
SUB = 8
LANES = 128
VMEM_LIMIT = 24 * 2**20
F32 = jnp.float32


def split_rows(cells):
    rows = cells.shape[-2] // SUB
    shaped = cells.reshape(cells.shape[:-2] + (SUB, rows, LANES))
    return jnp.swapaxes(shaped, -3, -2)


def join_rows(cells):
    rows = cells.shape[-3]
    return jnp.swapaxes(cells, -3, -2).reshape(cells.shape[:-3] + (rows * SUB, LANES))


def shapes(planes, rows):
    return jax.ShapeDtypeStruct((planes, rows, SUB, LANES), F32)


VMEM = pl.BlockSpec(memory_space=pltpu.VMEM)
SMEM = pl.BlockSpec(memory_space=pltpu.SMEM)
PARAMS = pltpu.CompilerParams(vmem_limit_bytes=VMEM_LIMIT)


def prepare(info, stacked, mine, other):
    slab, rows = stacked.shape[1], stacked.shape[2]
    wide, narrow = slab + 8, slab + 6

    def kernel(info_ref, own_ref, mine_ref, other_ref, cou_ref, a1, i1, a4, i4, q_ref):
        core = info_ref[0]
        low = info_ref[1].astype(F32)
        high = info_ref[2].astype(F32)

        def place(field, refs, index):
            into = (lambda p, value: cou_ref.__setitem__((field, p), value)) if field < 3 else (
                lambda p, value: q_ref.__setitem__(p, value)
            )
            for p in range(4):
                into(p, refs[0, index, p] * low)
                into(slab + 4 + p, refs[1, index, p] * high)

        for p in range(slab):
            for field in range(3):
                cou_ref[field, p + 4] = own_ref[field, p]
            q_ref[p + 4] = own_ref[3, p]

        @pl.when(core == 0)
        def _():
            for field in range(4):
                place(field, mine_ref if field < 2 else other_ref, field % 2)

        @pl.when(core == 1)
        def _():
            for field in range(4):
                place(field, other_ref if field < 2 else mine_ref, field % 2)

        for p in range(narrow):
            scale = low if p < 3 else (high if p >= slab + 3 else 1.0)
            for factor, a_ref, i_ref in ((1.0, a1, i1), (float(STEPS_DEV), a4, i4)):
                q = factor * q_ref[p + 1]
                inverse = scale / (1.0 + 6.0 * q)
                i_ref[p] = inverse
                a_ref[p] = q * inverse

    return pl.pallas_call(
        kernel,
        out_shape=(jax.ShapeDtypeStruct((3, wide, rows, SUB, LANES), F32),) + (shapes(narrow, rows),) * 4,
        in_specs=[SMEM, VMEM, VMEM, VMEM],
        out_specs=(VMEM,) * 5,
        scratch_shapes=[pltpu.VMEM((wide, rows, SUB, LANES), F32)],
        compiler_params=PARAMS,
        name="prepare",
    )(info, stacked, mine, other)


@functools.partial(jax.jit, static_argnames=("factor", "kind"))
def step(info, own, lower, upper, courant, a, inverse, factor, extra=None, kind="plain"):
    slab, rows = own.shape[0], own.shape[1]
    edge = SWEEPS + 1
    total = slab + 2 * edge

    def kernel(info_ref, own_ref, lo_ref, hi_ref, cou, a_ref, inv_ref, *rest):
        if kind == "plain":
            out, head, tail, u, v, w, b = rest
        elif kind == "less":
            extra_ref, out, u, v, w, b = rest
        else:
            extra_ref, out, head, tail, slot, u, v, w, b = rest
        lane = lax.broadcasted_iota(jnp.int32, (SUB, LANES), 1)
        sub = lax.broadcasted_iota(jnp.int32, (SUB, LANES), 0)
        first_lane, last_lane = lane == 0, lane == LANES - 1
        first_sub, last_sub = sub == 0, sub == SUB - 1
        low = info_ref[1].astype(F32)
        high = info_ref[2].astype(F32)

        def sides(x):
            left = jnp.where(first_lane, 0.0, pltpu.roll(x, 1, 1))
            right = jnp.where(last_lane, 0.0, pltpu.roll(x, LANES - 1, 1))
            return left, right

        def column(ref, z):
            xs = [ref[z, r] for r in range(rows)]
            top = jnp.where(first_sub, 0.0, pltpu.roll(xs[-1], 1, 0))
            bottom = jnp.where(last_sub, 0.0, pltpu.roll(xs[0], SUB - 1, 0))
            return [top] + xs + [bottom]

        for p in range(edge):
            u[p] = lo_ref[p] * low
            u[edge + slab + p] = hi_ref[p] * high
        for p in range(slab):
            u[edge + p] = own_ref[p]

        for z in range(1, total - 1):
            xs = column(u, z)
            for r in range(rows):
                x = xs[r + 1]
                left, right = sides(x)
                c = cou[0, z - 1, r]
                t = c * jnp.where(c > 0.0, x - u[z - 1, r], u[z + 1, r] - x)
                c = cou[1, z - 1, r]
                t = t + c * jnp.where(c > 0.0, x - xs[r], xs[r + 2] - x)
                c = cou[2, z - 1, r]
                t = t + c * jnp.where(c > 0.0, x - left, right - x)
                v[z, r] = x - factor * t

        src, dst = v, w
        for k in range(SWEEPS):
            for z in range(2 + k, total - 2 - k):
                xs = column(src, z)
                for r in range(rows):
                    x = xs[r + 1]
                    left, right = sides(x)
                    around = (left + right) + (xs[r] + xs[r + 2]) + (src[z - 1, r] + src[z + 1, r])
                    if k == 0:
                        base = inv_ref[z - 2, r] * x
                        b[z - 2, r] = base
                    else:
                        base = b[z - 2, r]
                    value = base + a_ref[z - 2, r] * around
                    if k < SWEEPS - 1:
                        dst[z, r] = value
                        continue
                    p = z - edge
                    if kind == "less":
                        value = value - extra_ref[p, r]
                    elif kind == "ring":
                        value = value + extra_ref[p, r]
                    out[p, r] = value
            src, dst = dst, src

        if kind != "less":
            head[...] = out[0:edge]
            tail[...] = out[slab - edge : slab]
        if kind == "ring":
            at_start = info_ref[3] == 1

            @pl.when(at_start)
            def _():
                slot[...] = out[...]

            @pl.when(jnp.logical_not(at_start))
            def _():
                slot[...] = extra_ref[...]

    outs = [shapes(slab, rows)]
    if kind != "less":
        outs += [shapes(edge, rows)] * 2
    if kind == "ring":
        outs += [shapes(slab, rows)]
    operands = [info, own, lower, upper, courant, a, inverse] + ([] if extra is None else [extra])
    return pl.pallas_call(
        kernel,
        out_shape=tuple(outs),
        in_specs=[SMEM] + [VMEM] * (len(operands) - 1),
        out_specs=(VMEM,) * len(outs),
        scratch_shapes=[pltpu.VMEM((total, rows, SUB, LANES), F32)] * 3
        + [pltpu.VMEM((total - 4, rows, SUB, LANES), F32)],
        compiler_params=PARAMS,
        cost_estimate=pl.CostEstimate(flops=16 * 2**20, bytes_accessed=6 * 2**20, transcendentals=0),
        name="step_" + kind,
    )(*operands)


def routes(points, slabs):
    def route(move):
        pairs = []
        for t in range(points):
            for s in range(slabs):
                to_t, to_s = move(t, s)
                pairs.append((t * slabs + s, (to_t % points) * slabs + to_s % slabs))
        return pairs

    def halo_of_start(shift, cycle):
        def move(t, s):
            if t == 0:
                return 0, s + shift
            return cycle.get(t, t ^ 1), s

        return route(move)

    ahead = {1: 2, 2: 3, 3: 1}
    behind = {1: points - 2, points - 2: points - 1, points - 1: 1}
    return {
        "later": route(lambda t, s: (t + 1, s)),
        "later_up": route(lambda t, s: (t + 1, s + 1)),
        "later_down": route(lambda t, s: (t + 1, s - 1)),
        "start_up": halo_of_start(1, ahead),
        "start_down": halo_of_start(-1, behind),
    }


def per_device(initial, guess, courant, diffusion, inflow):
    slabs = lax.axis_size("space")
    points = lax.axis_size("tm")
    edge = SWEEPS + 1
    both = ("tm", "space")
    route = routes(points, slabs)
    up = [(i, (i + 1) % slabs) for i in range(slabs)]
    down = [((i + 1) % slabs, i) for i in range(slabs)]
    earlier = [((i + 1) % points, i) for i in range(points)]
    partner = [(i, i ^ 1) for i in range(points)]
    ring = [(i, (i - 2 if i % 2 == 0 else i + 2) % points) for i in range(points)]
    leave = [(i, (i - 1 if i % 2 == 0 else i + 1) % points) for i in range(points)]

    place = lax.axis_index("space")
    time_place = lax.axis_index("tm")
    core = time_place % 2
    at_start = time_place == 0
    info = jnp.stack([core, place > 0, place < slabs - 1, at_start]).astype(jnp.int32)

    def halos(head, tail):
        return lax.ppermute(tail, "space", up), lax.ppermute(head, "space", down)

    def start_halos(head, tail):
        return (
            lax.ppermute(tail, both, route["start_up"]),
            lax.ppermute(head, both, route["start_down"]),
        )

    source = split_rows(jnp.where(time_place == points - 1, initial, guess[0]))
    slab = source.shape[0]

    stacked = split_rows(jnp.concatenate([courant, diffusion[None]], axis=0))
    half = lax.dynamic_slice_in_dim(stacked, 2 * core, 2, axis=0)
    half, source = lax.optimization_barrier((half, source))
    state = lax.ppermute(source, both, route["later"])
    lo = lax.ppermute(source[slab - edge :], both, route["later_up"])
    hi = lax.ppermute(source[:edge], both, route["later_down"])
    below, above = halos(half[:, :4], half[:, slab - 4 :])
    below, above, state, lo, hi = lax.optimization_barrier((below, above, state, lo, hi))
    mine = jnp.stack([below, above])
    other = lax.ppermute(mine, "tm", partner)
    cou, a1, i1, a4, i4 = prepare(info, stacked, mine, other)

    inflow = split_rows(inflow)

    for turn in range(STEPS_DEV):
        state, head, tail = step(info, state, lo, hi, cou, a1, i1, 1.0)
        if turn == 0:
            head, inflow = lax.optimization_barrier((head, inflow))
            error_lo, error_hi = start_halos(inflow[:edge], inflow[slab - edge :])
        lo, hi = halos(head, tail)
        if turn == 1:
            lo, hi, error_lo, error_hi = lax.optimization_barrier((lo, hi, error_lo, error_hi))
    relaxed = state
    relaxed_later = lax.ppermute(relaxed, "tm", earlier)

    second_pass = relaxed
    first_residual = second_pass - relaxed
    coarse = float(STEPS_DEV)
    error, head, tail, _ = step(
        info, inflow, error_lo, error_hi, cou, a4, i4, coarse, first_residual, "ring"
    )
    first_error = error
    error_lo, error_hi = start_halos(head, tail)

    for turn in range(STEPS_DEV - 1):
        state, head, tail = step(info, state, lo, hi, cou, a1, i1, 1.0)
        lo, hi = halos(head, tail)
    lo, hi, error_lo, error_hi = lax.optimization_barrier((lo, hi, error_lo, error_hi))
    (odd,) = step(info, state, lo, hi, cou, a1, i1, 1.0, relaxed_later, "less")
    even = lax.ppermute(odd, "tm", earlier)
    residual = lax.ppermute(odd, both, route["later"])

    for turn in range(1, points):
        slot = odd if turn % 2 else even
        error, head, tail, slot = step(
            info, error, error_lo, error_hi, cou, a4, i4, coarse, slot, "ring"
        )
        if turn < points - 1:
            error_lo, error_hi = start_halos(head, tail)
            if turn == 3:
                residual, slot, error_lo, error_hi = lax.optimization_barrier(
                    (residual, slot, error_lo, error_hi)
                )
            else:
                slot, error_lo, error_hi = lax.optimization_barrier((slot, error_lo, error_hi))
            slot = lax.ppermute(slot, "tm", ring)
        else:
            slot = lax.ppermute(slot, "tm", leave)
        if turn % 2:
            odd = slot
        else:
            even = slot
    residual = jnp.where(at_start, first_residual, residual)
    error = jnp.where(at_start, first_error, jnp.where(core == 1, odd, even))
    return join_rows(relaxed + error)[None], join_rows(residual)[None]


def solution(mesh):
    in_specs = (
        P("space", None, None),
        P("tm", "space", None, None),
        P(None, "space", None, None),
        P("space", None, None),
        P("space", None, None),
    )
    out_specs = (P("tm", "space", None, None), P("tm", "space", None, None))
    return jax.shard_map(
        per_device, mesh=mesh, in_specs=in_specs, out_specs=out_specs, check_vma=False
    )
```

```python
import functools

import jax
import jax.numpy as jnp
from jax import lax
from jax.experimental import pallas as pl
from jax.experimental.pallas import tpu as pltpu
from jax.sharding import PartitionSpec as P

STEPS_DEV = 4
SWEEPS = 4
SUB = 8
LANES = 128
VMEM_LIMIT = 24 * 2**20
F32 = jnp.float32


def split_rows(cells):
    rows = cells.shape[-2] // SUB
    shaped = cells.reshape(cells.shape[:-2] + (SUB, rows, LANES))
    return jnp.swapaxes(shaped, -3, -2)


def join_rows(cells):
    rows = cells.shape[-3]
    return jnp.swapaxes(cells, -3, -2).reshape(cells.shape[:-3] + (rows * SUB, LANES))


def shapes(planes, rows):
    return jax.ShapeDtypeStruct((planes, rows, SUB, LANES), F32)


VMEM = pl.BlockSpec(memory_space=pltpu.VMEM)
SMEM = pl.BlockSpec(memory_space=pltpu.SMEM)
PARAMS = pltpu.CompilerParams(vmem_limit_bytes=VMEM_LIMIT)


def prepare(info, stacked, mine, other):
    slab, rows = stacked.shape[1], stacked.shape[2]
    wide, narrow = slab + 8, slab + 6

    def kernel(info_ref, own_ref, mine_ref, other_ref, cou_ref, a1, i1, a4, i4, q_ref):
        core = info_ref[0]
        low = info_ref[1].astype(F32)
        high = info_ref[2].astype(F32)

        def place(field, refs, index):
            into = (lambda p, value: cou_ref.__setitem__((field, p), value)) if field < 3 else (
                lambda p, value: q_ref.__setitem__(p, value)
            )
            for p in range(4):
                into(p, refs[0, index, p] * low)
                into(slab + 4 + p, refs[1, index, p] * high)

        for p in range(slab):
            for field in range(3):
                cou_ref[field, p + 4] = own_ref[field, p]
            q_ref[p + 4] = own_ref[3, p]

        @pl.when(core == 0)
        def _():
            for field in range(4):
                place(field, mine_ref if field < 2 else other_ref, field % 2)

        @pl.when(core == 1)
        def _():
            for field in range(4):
                place(field, other_ref if field < 2 else mine_ref, field % 2)

        for p in range(narrow):
            scale = low if p < 3 else (high if p >= slab + 3 else 1.0)
            for factor, a_ref, i_ref in ((1.0, a1, i1), (float(STEPS_DEV), a4, i4)):
                q = factor * q_ref[p + 1]
                inverse = scale / (1.0 + 6.0 * q)
                i_ref[p] = inverse
                a_ref[p] = q * inverse

    return pl.pallas_call(
        kernel,
        out_shape=(jax.ShapeDtypeStruct((3, wide, rows, SUB, LANES), F32),) + (shapes(narrow, rows),) * 4,
        in_specs=[SMEM, VMEM, VMEM, VMEM],
        out_specs=(VMEM,) * 5,
        scratch_shapes=[pltpu.VMEM((wide, rows, SUB, LANES), F32)],
        compiler_params=PARAMS,
        name="prepare",
    )(info, stacked, mine, other)


@functools.partial(jax.jit, static_argnames=("factor", "kind"))
def step(info, own, lower, upper, courant, a, inverse, factor, extra=None, kind="plain"):
    slab, rows = own.shape[0], own.shape[1]
    edge = SWEEPS + 1
    total = slab + 2 * edge

    def kernel(info_ref, own_ref, lo_ref, hi_ref, cou, a_ref, inv_ref, *rest):
        if kind == "plain":
            out, head, tail, u, v, w, b = rest
        elif kind == "less":
            extra_ref, out, u, v, w, b = rest
        else:
            extra_ref, out, head, tail, slot, u, v, w, b = rest
        lane = lax.broadcasted_iota(jnp.int32, (SUB, LANES), 1)
        sub = lax.broadcasted_iota(jnp.int32, (SUB, LANES), 0)
        first_lane, last_lane = lane == 0, lane == LANES - 1
        first_sub, last_sub = sub == 0, sub == SUB - 1
        low = info_ref[1].astype(F32)
        high = info_ref[2].astype(F32)

        def sides(x):
            left = jnp.where(first_lane, 0.0, pltpu.roll(x, 1, 1))
            right = jnp.where(last_lane, 0.0, pltpu.roll(x, LANES - 1, 1))
            return left, right

        def column(plane):
            xs = [plane[r] for r in range(rows)]
            top = jnp.where(first_sub, 0.0, pltpu.roll(xs[-1], 1, 0))
            bottom = jnp.where(last_sub, 0.0, pltpu.roll(xs[0], SUB - 1, 0))
            return [top] + xs + [bottom]

        for p in range(edge):
            u[p] = lo_ref[p] * low
            u[edge + slab + p] = hi_ref[p] * high

        def state(z):
            return own_ref.at[z - edge] if edge <= z < edge + slab else u.at[z]

        for z in range(1, total - 1):
            xs = column(state(z))
            under, over = state(z - 1), state(z + 1)
            for r in range(rows):
                x = xs[r + 1]
                left, right = sides(x)
                c = cou[0, z - 1, r]
                t = c * jnp.where(c > 0.0, x - under[r], over[r] - x)
                c = cou[1, z - 1, r]
                t = t + c * jnp.where(c > 0.0, x - xs[r], xs[r + 2] - x)
                c = cou[2, z - 1, r]
                t = t + c * jnp.where(c > 0.0, x - left, right - x)
                v[z, r] = x - factor * t

        src, dst = v, w
        for k in range(SWEEPS):
            for z in range(2 + k, total - 2 - k):
                xs = column(src.at[z])
                for r in range(rows):
                    x = xs[r + 1]
                    left, right = sides(x)
                    around = (left + right) + (xs[r] + xs[r + 2]) + (src[z - 1, r] + src[z + 1, r])
                    if k == 0:
                        base = inv_ref[z - 2, r] * x
                        b[z - 2, r] = base
                    else:
                        base = b[z - 2, r]
                    value = base + a_ref[z - 2, r] * around
                    if k < SWEEPS - 1:
                        dst[z, r] = value
                        continue
                    p = z - edge
                    if kind == "less":
                        value = value - extra_ref[p, r]
                    elif kind == "ring":
                        value = value + extra_ref[p, r]
                    out[p, r] = value
            src, dst = dst, src

        if kind != "less":
            head[...] = out[0:edge]
            tail[...] = out[slab - edge : slab]
        if kind == "ring":
            at_start = info_ref[3] == 1

            @pl.when(at_start)
            def _():
                slot[...] = out[...]

            @pl.when(jnp.logical_not(at_start))
            def _():
                slot[...] = extra_ref[...]

    outs = [shapes(slab, rows)]
    if kind != "less":
        outs += [shapes(edge, rows)] * 2
    if kind == "ring":
        outs += [shapes(slab, rows)]
    operands = [info, own, lower, upper, courant, a, inverse] + ([] if extra is None else [extra])
    return pl.pallas_call(
        kernel,
        out_shape=tuple(outs),
        in_specs=[SMEM] + [VMEM] * (len(operands) - 1),
        out_specs=(VMEM,) * len(outs),
        scratch_shapes=[pltpu.VMEM((total, rows, SUB, LANES), F32)] * 3
        + [pltpu.VMEM((total - 4, rows, SUB, LANES), F32)],
        compiler_params=PARAMS,
        cost_estimate=pl.CostEstimate(flops=16 * 2**20, bytes_accessed=6 * 2**20, transcendentals=0),
        name="step_" + kind,
    )(*operands)


def routes(points, slabs):
    def route(move):
        pairs = []
        for t in range(points):
            for s in range(slabs):
                to_t, to_s = move(t, s)
                pairs.append((t * slabs + s, (to_t % points) * slabs + to_s % slabs))
        return pairs

    def halo_of_start(shift, cycle):
        def move(t, s):
            if t == 0:
                return 0, s + shift
            return cycle.get(t, t ^ 1), s

        return route(move)

    ahead = {1: 2, 2: 3, 3: 1}
    behind = {1: points - 2, points - 2: points - 1, points - 1: 1}
    return {
        "later": route(lambda t, s: (t + 1, s)),
        "later_up": route(lambda t, s: (t + 1, s + 1)),
        "later_down": route(lambda t, s: (t + 1, s - 1)),
        "start_up": halo_of_start(1, ahead),
        "start_down": halo_of_start(-1, behind),
    }


def per_device(initial, guess, courant, diffusion, inflow):
    slabs = lax.axis_size("space")
    points = lax.axis_size("tm")
    edge = SWEEPS + 1
    both = ("tm", "space")
    route = routes(points, slabs)
    up = [(i, (i + 1) % slabs) for i in range(slabs)]
    down = [((i + 1) % slabs, i) for i in range(slabs)]
    earlier = [((i + 1) % points, i) for i in range(points)]
    partner = [(i, i ^ 1) for i in range(points)]
    ring = [(i, (i - 2 if i % 2 == 0 else i + 2) % points) for i in range(points)]
    leave = [(i, (i - 1 if i % 2 == 0 else i + 1) % points) for i in range(points)]

    place = lax.axis_index("space")
    time_place = lax.axis_index("tm")
    core = time_place % 2
    at_start = time_place == 0
    info = jnp.stack([core, place > 0, place < slabs - 1, at_start]).astype(jnp.int32)

    def halos(head, tail):
        return lax.ppermute(tail, "space", up), lax.ppermute(head, "space", down)

    def start_halos(head, tail):
        return (
            lax.ppermute(tail, both, route["start_up"]),
            lax.ppermute(head, both, route["start_down"]),
        )

    source = split_rows(jnp.where(time_place == points - 1, initial, guess[0]))
    slab = source.shape[0]

    stacked = split_rows(jnp.concatenate([courant, diffusion[None]], axis=0))
    half = lax.dynamic_slice_in_dim(stacked, 2 * core, 2, axis=0)
    half, source = lax.optimization_barrier((half, source))
    state = lax.ppermute(source, both, route["later"])
    lo = lax.ppermute(source[slab - edge :], both, route["later_up"])
    hi = lax.ppermute(source[:edge], both, route["later_down"])
    below, above = halos(half[:, :4], half[:, slab - 4 :])
    below, above, state, lo, hi = lax.optimization_barrier((below, above, state, lo, hi))
    mine = jnp.stack([below, above])
    other = lax.ppermute(mine, "tm", partner)
    cou, a1, i1, a4, i4 = prepare(info, stacked, mine, other)

    inflow = split_rows(inflow)

    for turn in range(STEPS_DEV):
        state, head, tail = step(info, state, lo, hi, cou, a1, i1, 1.0)
        if turn == 0:
            head, inflow = lax.optimization_barrier((head, inflow))
            error_lo, error_hi = start_halos(inflow[:edge], inflow[slab - edge :])
        lo, hi = halos(head, tail)
        if turn == 1:
            lo, hi, error_lo, error_hi = lax.optimization_barrier((lo, hi, error_lo, error_hi))
    relaxed = state
    relaxed_later = lax.ppermute(relaxed, "tm", earlier)

    second_pass = relaxed
    first_residual = second_pass - relaxed
    coarse = float(STEPS_DEV)
    error, head, tail, _ = step(
        info, inflow, error_lo, error_hi, cou, a4, i4, coarse, first_residual, "ring"
    )
    first_error = error
    error_lo, error_hi = start_halos(head, tail)

    for turn in range(STEPS_DEV - 1):
        state, head, tail = step(info, state, lo, hi, cou, a1, i1, 1.0)
        lo, hi = halos(head, tail)
    lo, hi, error_lo, error_hi = lax.optimization_barrier((lo, hi, error_lo, error_hi))
    (odd,) = step(info, state, lo, hi, cou, a1, i1, 1.0, relaxed_later, "less")
    even = lax.ppermute(odd, "tm", earlier)
    residual = lax.ppermute(odd, both, route["later"])

    for turn in range(1, points):
        slot = odd if turn % 2 else even
        error, head, tail, slot = step(
            info, error, error_lo, error_hi, cou, a4, i4, coarse, slot, "ring"
        )
        if turn < points - 1:
            error_lo, error_hi = start_halos(head, tail)
            if turn == 3:
                residual, slot = lax.optimization_barrier((residual, slot))
                residual = join_rows(jnp.where(at_start, first_residual, residual))
            if turn == 5:
                residual, slot = lax.optimization_barrier((residual, slot))
            if turn == points - 2:
                slot = lax.ppermute(slot, "tm", ring)
            slot, error_lo, error_hi = lax.optimization_barrier((slot, error_lo, error_hi))
            if turn < points - 2:
                slot = lax.ppermute(slot, "tm", ring)
        else:
            slot = lax.ppermute(slot, "tm", leave)
        if turn % 2:
            odd = slot
        else:
            even = slot
    error = jnp.where(at_start, first_error, jnp.where(core == 1, odd, even))
    return join_rows(relaxed + error)[None], residual[None]


def solution(mesh):
    in_specs = (
        P("space", None, None),
        P("tm", "space", None, None),
        P(None, "space", None, None),
        P("space", None, None),
        P("space", None, None),
    )
    out_specs = (P("tm", "space", None, None), P("tm", "space", None, None))
    return jax.shard_map(
        per_device, mesh=mesh, in_specs=in_specs, out_specs=out_specs, check_vma=False
    )
```
